256 devices in a mesh: fsdp: 64 (over y, z, x_hi), tp: 4 (over x_lo, core).
Axes of the slice: x: 4 (x_hi: 2, x_lo: 2; x = x_hi * 2 + x_lo), y: 4, z: 8, core: 2. Of those that a mesh axis runs over, the one named last changes fastest.
Arguments:
- tokens_in: bfloat16 [98304, 5120], P(('fsdp', 'tp')), may hold values from -6 to 6
- cotangent: bfloat16 [98304, 2048], P('fsdp', 'tp'), may hold values from -6 to 6
- weight: bfloat16 [5120, 2048], P('fsdp', 'tp'), may hold values from -0.078125 to 0.078125
- hidden_rows: bfloat16 [256, 5120], P('fsdp'), may hold values from -6 to 6
- queries: bfloat16 [256, 5120], P('fsdp', 'tp')
- cache: bfloat16 [256, 1024, 2048], P('fsdp', None, 'tp')
- lengths: int32 [256], P('fsdp'), may hold values from 2 to 1024, as said below
Outputs:
- new_weight: bfloat16 [5120, 2048], P('fsdp', 'tp')
- attention: bfloat16 [256, 5120], P('fsdp', 'tp')
The draws below stay inside these ranges and needn't reach their ends.
Inputs may be any that keep to these rules, and one draw needn't show every extreme that they name: `lengths`: each row has at least two live positions; some row has all 1024 live.
All inputs are finite; a program needn't handle non-finite values.
Results may differ from the reference program's by a relative error of at most 0.007.
Values may be sent and summed in bfloat16 or wider, within the bound.
No kernel may reach another device: no remote copies, remote signals or barrier semaphores. Data moves between devices by JAX's collectives and lax.ppermute only.
A program may use at most 128 MiB of HBM per device.

```python
import math
import jax
import jax.numpy as jnp
from jax import lax

D = 5120
QH = 40
KVH = 8
HD = 128
CTX = 1024
TOKENS = 98304
ROWS = 256


def first_keys(key):
    return jax.random.normal(jax.random.fold_in(key, 13), (ROWS, KVH, HD), jnp.float32)


def draw_cache(key, part):
    anchor = first_keys(key)
    key = jax.random.fold_in(key, 1)
    stored = jax.random.normal(key, (ROWS, CTX, KVH, 2, HD), jnp.float32)
    stored = stored.at[:, 0, :, 0, :].set(anchor)
    return stored.reshape(ROWS, CTX, 2 * KVH * HD).astype(jnp.bfloat16)


def draw_queries(key, part):
    key = jax.random.fold_in(key, 2)
    drawn = jax.random.normal(key, (ROWS, QH, HD), jnp.float32)
    return drawn.reshape(ROWS, QH * HD).astype(jnp.bfloat16)


def draw_lengths(key, part):
    key = jax.random.fold_in(key, 3)
    counts = jax.random.randint(jax.random.fold_in(key, 1), (ROWS,), 2, CTX + 1)
    chosen = jax.random.randint(jax.random.fold_in(key, 2), (), 0, ROWS)
    return counts.at[chosen].set(CTX).astype(jnp.int32)


def steps_of(key, dims, pieces, least, largest):
    level = 1.0
    for axis_at, parts in pieces:
        heights = jax.random.uniform(jax.random.fold_in(jax.random.fold_in(key, 6), axis_at), (parts,), jnp.float32, least / len(pieces), largest / len(pieces))
        level = level * jnp.repeat(jnp.exp(heights), dims[axis_at] // parts).reshape((-1,) + (1,) * (len(dims) - 1 - axis_at))
    return level


def normal_values(key, dims, scale, bound, shards=(), kind=jnp.bfloat16):
    entries = jax.random.normal(key, dims, jnp.float32) * scale
    if len(shards) > 0:
        entries = steps_of(key, dims, shards, -0.22, 0.18) * entries
    return jnp.clip(entries, min=-bound, max=bound).astype(kind)


def setup_inputs(seed: int = 0) -> dict:
    keys = jax.random.split(jax.random.key(seed), 8)
    return {
        "tokens_in": normal_values(keys[0], (TOKENS, D), 1.0, 6.0, ((0, 256),)),
        "cotangent": normal_values(keys[1], (TOKENS, 2 * KVH * HD), 1.0, 6.0, ((0, 64), (1, 4))),
        "weight": normal_values(keys[2], (D, 2 * KVH * HD), D ** -0.5, 0.078125, ((0, 64), (1, 4))),
        "hidden_rows": normal_values(keys[3], (ROWS, D), 1.0, 6.0, ((0, 64),)),
        "queries": draw_queries(jax.random.fold_in(keys[7], 71), 0),
        "cache": draw_cache(jax.random.fold_in(keys[7], 71), 0),
        "lengths": draw_lengths(jax.random.fold_in(keys[7], 71), 0),
    }


def attend(queries, cache, fresh, lengths, heads_kv, head_size):
    rows = cache.shape[0]
    span = cache.shape[1]
    group = queries.shape[1] // (heads_kv * head_size)
    query = queries.reshape(rows, heads_kv, group, head_size).astype(jnp.float32)
    stored = cache.reshape(rows, span, heads_kv, 2, head_size).astype(jnp.float32)
    latest = fresh.reshape(rows, heads_kv, 2, head_size).astype(jnp.float32)
    scores = jnp.einsum('rjgd,rcjd->rjgc', query, stored[:, :, :, 0, :]) / math.sqrt(head_size)
    newest = jnp.einsum('rjgd,rjd->rjg', query, latest[:, :, 0, :]) / math.sqrt(head_size)
    live = jnp.arange(span, dtype=jnp.int32)[None, :] < lengths[:, None]
    scores = jnp.where(live[:, None, None, :], scores, jnp.float32(-1e+30))
    top = jnp.maximum(lax.optimization_barrier(jnp.max(scores, axis=-1)), newest)
    past_exp = jnp.exp(scores - top[..., None])
    new_exp = jnp.exp(newest - top)
    total = lax.optimization_barrier(jnp.sum(past_exp, axis=-1)) + new_exp
    past_prob = (past_exp / total[..., None]).astype(jnp.bfloat16).astype(jnp.float32)
    new_prob = (new_exp / total).astype(jnp.bfloat16).astype(jnp.float32)
    mixed = jnp.einsum('rjgc,rcjd->rjgd', past_prob, stored[:, :, :, 1, :])
    mixed = mixed + new_prob[..., None] * latest[:, :, None, 1, :]
    return mixed.reshape(rows, -1).astype(jnp.bfloat16)

def reference(tokens_in, cotangent, weight, hidden_rows, queries, cache, lengths):
    grad = jnp.dot(tokens_in.T, cotangent, preferred_element_type=jnp.float32)
    factor = 0.01 / math.sqrt(TOKENS)
    new_weight = (weight.astype(jnp.float32) - factor * grad).astype(jnp.bfloat16)
    fresh = jnp.dot(hidden_rows, new_weight, preferred_element_type=jnp.float32).astype(jnp.bfloat16)

    def one_row(items):
        return attend(items[0], items[1], items[2], items[3], KVH, HD)
    attention = lax.map(one_row, (queries[:, None], cache[:, None], fresh[:, None], lengths[:, None]))
    return (new_weight, attention.reshape(ROWS, QH * HD))
```

```python
import math

import jax
import jax.numpy as jnp
import numpy as np
from jax import lax
from jax.sharding import Mesh
from jax.sharding import PartitionSpec as P

KVH = 8
HD = 128
F32 = jnp.float32
BF16 = jnp.bfloat16
X = ("xh", "xl")


def shift(value, axis, size, by):
    return lax.ppermute(value, axis, [(i, (i + by) % size) for i in range(size)])


def ring_reduce(chunk, axis, size, near):
    half = size // 2
    total = chunk(0).astype(F32)
    for way, start in ((near, half), (-near, half - 1)):
        run = chunk(way * start)
        for step in range(start - 1, 0, -1):
            run = shift(run, axis, size, way)
            run = (run.astype(F32) + chunk(way * step).astype(F32)).astype(BF16)
        total = total + shift(run, axis, size, way).astype(F32)
    return total


def direct_reduce(chunk, axis, size):
    total = chunk(0).astype(F32)
    for by in range(1, size):
        total = total + shift(chunk(by), axis, size, by).astype(F32)
    return total


def attend(queries, cache, fresh, lengths, heads_kv, head_size):
    rows = cache.shape[0]
    span = cache.shape[1]
    group = queries.shape[1] // (heads_kv * head_size)
    query = queries.reshape(rows, heads_kv, group, head_size)
    stored = cache.reshape(rows, span, heads_kv, 2, head_size)
    latest = fresh.reshape(rows, heads_kv, 2, head_size)
    scores = jnp.einsum(
        "rjgd,rcjd->rjgc", query, stored[:, :, :, 0, :], preferred_element_type=jnp.float32
    ) / math.sqrt(head_size)
    newest = jnp.einsum(
        "rjgd,rjd->rjg", query, latest[:, :, 0, :], preferred_element_type=jnp.float32
    ) / math.sqrt(head_size)
    live = jnp.arange(span, dtype=jnp.int32)[None, :] < lengths[:, None]
    scores = jnp.where(live[:, None, None, :], scores, jnp.float32(-1e30))
    top = jnp.maximum(jnp.max(scores, axis=-1), newest)
    past_exp = jnp.exp(scores - top[..., None])
    new_exp = jnp.exp(newest - top)
    total = jnp.sum(past_exp, axis=-1) + new_exp
    past_prob = (past_exp / total[..., None]).astype(jnp.bfloat16)
    new_prob = (new_exp / total).astype(jnp.bfloat16)
    mixed = jnp.einsum(
        "rjgc,rcjd->rjgd", past_prob, stored[:, :, :, 1, :], preferred_element_type=jnp.float32
    )
    mixed = mixed + new_prob.astype(jnp.float32)[..., None] * latest[:, :, None, 1, :].astype(
        jnp.float32
    )
    return mixed.reshape(rows, -1).astype(jnp.bfloat16)


def pick(array, index):
    return lax.dynamic_index_in_dim(array, index, 0, keepdims=False)


def product(tokens, cotangent):
    return lax.dot_general(
        tokens, cotangent, (((0,), (0,)), ((), ())), preferred_element_type=jnp.float32
    )


def local(tokens_in, cotangent, weight, hidden_rows, queries, cache, lengths):
    y, z, xh, xl, c = (lax.axis_index(name) for name in ("y", "z", "xh", "xl", "c"))
    ny, nz, nh, nl, nc = (lax.axis_size(name) for name in ("y", "z", "xh", "xl", "c"))
    x = xh * nl + xl
    nx = nh * nl
    tokens, width = tokens_in.shape
    columns = cotangent.shape[1]
    part = columns // 2
    rows = weight.shape[0]

    other_tokens = shift(tokens_in, "c", nc, 1)
    blocks = cotangent.reshape(nl, nc, tokens, columns)
    mine = pick(blocks, xl)
    got = shift(pick(blocks, 1 - xl), "xl", nl, 1)
    grads = []
    for block in (mine, got):
        grads.append(
            (product(tokens_in, pick(block, c)) + product(other_tokens, pick(block, 1 - c))).astype(BF16)
        )

    first = [g[:, :part].reshape(ny, nz, nh, rows, part) for g in grads]
    after = []
    for values, near in zip(first, (1, -1)):
        after.append(
            ring_reduce(lambda k, v=values: pick(v, (y + k) % ny), "y", ny, near).astype(BF16)
        )

    def to_x(k):
        values = after[k % 2]
        return lax.dynamic_index_in_dim(values, ((x + k) % nx) // nl, 1, keepdims=False)

    summed = direct_reduce(to_x, X, nx).astype(BF16)
    grad_first = direct_reduce(lambda k: pick(summed, (z + k) % nz), "z", nz)

    second = [g[:, part:].reshape(ny, nz, nh * rows, part) for g in grads]
    after_z = []
    for values, near in zip(second, (1, -1)):
        after_z.append(
            ring_reduce(
                lambda k, v=values: lax.dynamic_index_in_dim(v, (z + k) % nz, 1, keepdims=False),
                "z",
                nz,
                near,
            ).astype(BF16)
        )
    both = jnp.stack(after_z, 1)
    summed_y = direct_reduce(lambda k: pick(both, (y + k) % ny), "y", ny).astype(BF16)
    by_x = summed_y.reshape(2, nh, rows, part)
    grad_second = direct_reduce(lambda k: pick(by_x[k % 2], ((x + k) % nx) // nl), X, nx)

    grad = jnp.concatenate([grad_first, grad_second], axis=1)
    total_tokens = tokens * nc * nl * nh * ny * nz
    factor = 0.01 / math.sqrt(total_tokens)
    new_weight = (weight.astype(jnp.float32) - factor * grad).astype(jnp.bfloat16)
    gathered = lax.all_gather(new_weight, ("y", "z", "xh"), axis=0, tiled=True)
    fresh = jnp.dot(hidden_rows, gathered, preferred_element_type=jnp.float32).astype(jnp.bfloat16)
    attention = attend(queries, cache, fresh, lengths, KVH // (nl * nc), HD)
    return (new_weight, attention)


def solution(mesh):
    names = ("y", "z", "xh", "xl", "c")
    fine = Mesh(np.asarray(mesh.devices).reshape(4, 8, 2, 2, 2), names)
    fsdp, tp = names[:3], names[3:]
    in_specs = (
        P(names, None),
        P(fsdp, tp),
        P(fsdp, tp),
        P(fsdp, None),
        P(fsdp, tp),
        P(fsdp, None, tp),
        P(fsdp),
    )
    out_specs = (P(fsdp, tp), P(fsdp, tp))
    return jax.shard_map(local, mesh=fine, in_specs=in_specs, out_specs=out_specs, check_vma=False)
```

```python
import functools
import math

import jax
import jax.numpy as jnp
import numpy as np
from jax import lax
from jax.experimental import pallas as pl
from jax.experimental.pallas import tpu as pltpu
from jax.sharding import Mesh
from jax.sharding import PartitionSpec as P

KVH = 8
HD = 128
F32 = jnp.float32
BF16 = jnp.bfloat16
X = ("xh", "xl")
VMEM = pl.BlockSpec(memory_space=pltpu.VMEM)


def shift(value, axis, size, by):
    return lax.ppermute(value, axis, [(i, (i + by) % size) for i in range(size)])


def swap(value, axis, size, bits):
    return lax.ppermute(value, axis, [(i, i ^ bits) for i in range(size)])


def pick(array, index, axis=0):
    return lax.dynamic_index_in_dim(array, index, axis, keepdims=False)


def add(a, b):
    return (a.astype(F32) + b.astype(F32)).astype(BF16)


def product_kernel(split, rows, place, a_ref, b_ref, ca_ref, cb_ref, *outs):
    by_y, by_x = outs[:4], outs[4:]
    turn = pl.program_id(0)
    contract = (((0,), (0,)), ((), ()))
    total = lax.dot_general(a_ref[...], ca_ref[...], contract, preferred_element_type=F32)
    total += lax.dot_general(b_ref[...], cb_ref[...], contract, preferred_element_type=F32)
    total = total.astype(BF16)
    part = total.shape[1] // 2
    for k in range(4):

        @pl.when(turn == k)
        def _(k=k):
            by_y[k][...] = total[:, :part]

    def store(near, far):
        for i in range(total.shape[0] // (2 * rows)):
            here = slice(i * rows, (i + 1) * rows)
            for target, at in ((near, 2 * i), (far, 2 * i + 1)):
                for out in target:
                    out[here, :] = total[at * rows : (at + 1) * rows, part:]

    first = place[1]
    if split:
        for low in (True, False):
            for flip in (0, 1):

                @pl.when(((turn < 2) == low) & (first == flip))
                def _(low=low, flip=flip):
                    pair = ((by_x[0],), (by_x[1] if low else by_x[2],))
                    store(*(pair if flip == 0 else pair[::-1]))
    else:
        for flip in (0, 1):

            @pl.when(first == flip)
            def _(flip=flip):
                pair = ((by_x[0],), (by_x[1],))
                store(*(pair if flip == 0 else pair[::-1]))


def product(split, rows, place, own, other, own_cot, other_cot):
    tokens, width = own.shape
    columns = own_cot.shape[1]
    part = columns // 2
    steps = 2
    tall = width // (4 * steps)

    def within(first, last):
        def index(turn, step, place):
            at = (turn - first) * steps + step
            return (jnp.clip(at, 0, (last - first) * steps - 1), 0)

        return index

    token_spec = pl.BlockSpec((tokens, tall), lambda t, s, place: (0, ((place[0] + t) % 4) * steps + s))
    whole = pl.BlockSpec((tokens, columns), lambda t, s, place: (0, 0))
    y_specs = [pl.BlockSpec((tall, part), within(k, k + 1)) for k in range(4)]
    y_shapes = [jax.ShapeDtypeStruct((width // 4, part), BF16)] * 4
    spans = ((0, 4), (0, 2), (2, 4)) if split else ((0, 4), (0, 4))
    x_specs = [pl.BlockSpec((tall // 2, part), within(*span)) for span in spans]
    x_shapes = [jax.ShapeDtypeStruct((width // 8 * (b - a), part), BF16) for a, b in spans]
    return pl.pallas_call(
        functools.partial(product_kernel, split, rows),
        grid_spec=pltpu.PrefetchScalarGridSpec(
            num_scalar_prefetch=1,
            grid=(4, steps),
            in_specs=[token_spec, token_spec, whole, whole],
            out_specs=y_specs + x_specs,
        ),
        out_shape=y_shapes + x_shapes,
        compiler_params=pltpu.CompilerParams(vmem_limit_bytes=24 << 20),
        cost_estimate=pl.CostEstimate(
            flops=4 * tokens * width * columns, bytes_accessed=6 * tokens * width, transcendentals=0
        ),
        name="product",
    )(place, own, other, own_cot, other_cot)


def past_kernel(heads, lengths, query_ref, cache_ref, sum_ref, top_ref, mass_ref):
    span = cache_ref.shape[1]
    live = lax.broadcasted_iota(jnp.int32, (8, span), 1) < lengths[pl.program_id(0)]
    for j in range(heads):
        keys = cache_ref[0, :, 2 * j * HD : (2 * j + 1) * HD]
        values = cache_ref[0, :, (2 * j + 1) * HD : (2 * j + 2) * HD]
        scores = lax.dot_general(
            query_ref[0, j], keys, (((1,), (1,)), ((), ())), preferred_element_type=F32
        ) / math.sqrt(HD)
        scores = jnp.where(live, scores, jnp.float32(-1e30))
        top = jnp.max(scores, axis=1, keepdims=True)
        weights = jnp.exp(scores - top)
        mass = jnp.sum(weights, axis=1, keepdims=True)
        sum_ref[0, j] = jnp.dot(weights.astype(BF16), values, preferred_element_type=F32)
        top_ref[0, j] = jnp.broadcast_to(top, (8, HD))
        mass_ref[0, j] = jnp.broadcast_to(mass, (8, HD))


def attend_past(query, cache, lengths):
    rows, heads = query.shape[:2]
    span, columns = cache.shape[1:]
    small = pl.BlockSpec((1, heads, 8, HD), lambda r, lengths: (r, 0, 0, 0))
    shape = jax.ShapeDtypeStruct((rows, heads, 8, HD), F32)
    return pl.pallas_call(
        functools.partial(past_kernel, heads),
        grid_spec=pltpu.PrefetchScalarGridSpec(
            num_scalar_prefetch=1,
            grid=(rows,),
            in_specs=[small, pl.BlockSpec((1, span, columns), lambda r, lengths: (r, 0, 0))],
            out_specs=[small] * 3,
        ),
        out_shape=[shape] * 3,
        compiler_params=pltpu.CompilerParams(vmem_limit_bytes=16 << 20),
        cost_estimate=pl.CostEstimate(
            flops=32 * rows * span * columns,
            bytes_accessed=2 * rows * span * columns,
            transcendentals=8 * rows * heads * span,
        ),
        name="past",
    )(lengths, query, cache)


def finish_kernel(factor, rows, weight_ref, query_ref, sum_ref, top_ref, mass_ref, *refs):
    parts, (weight_out, attention_out) = refs[:-2], refs[-2:]
    total = parts[0][...].astype(F32)
    for ref in parts[1:]:
        total += ref[...].astype(F32)
    weight_out[...] = (weight_ref[...].astype(F32) - factor * total[:rows]).astype(BF16)
    fresh = total[rows:].astype(BF16).astype(F32)
    for r in range(query_ref.shape[0]):
        for j in range(query_ref.shape[1]):
            key = fresh[r : r + 1, 2 * j * HD : (2 * j + 1) * HD]
            value = fresh[r : r + 1, (2 * j + 1) * HD : (2 * j + 2) * HD]
            newest = jnp.sum(query_ref[r, j].astype(F32) * key, axis=1, keepdims=True) / math.sqrt(HD)
            old = top_ref[r, j]
            top = jnp.maximum(old, newest)
            past = jnp.exp(old - top)
            new = jnp.exp(newest - top)
            mixed = (sum_ref[r, j] * past + new * value) / (mass_ref[r, j] * past + new)
            attention_out[r, j] = mixed.astype(BF16)


def local(tokens_in, cotangent, weight, hidden_rows, queries, cache, lengths):
    y, z, xh, xl, c = (lax.axis_index(name) for name in ("y", "z", "xh", "xl", "c"))
    ny, nz, nh, nl, nc = (lax.axis_size(name) for name in ("y", "z", "xh", "xl", "c"))
    x = xh * nl + xl
    nx = nh * nl
    tokens, width = tokens_in.shape
    columns = cotangent.shape[1]
    part = columns // 2
    rows = weight.shape[0]
    factor = 0.01 / math.sqrt(tokens * nc * nl * nh * ny * nz)

    other_tokens = swap(tokens_in, "c", nc, 1)
    blocks = cotangent.reshape(nl, nc, tokens, columns)
    mine = pick(blocks, xl)
    got = swap(pick(blocks, 1 - xl), "xl", nl, 1)
    cots = [(pick(block, c), pick(block, 1 - c)) for block in (mine, got)]

    near_half = pick(hidden_rows.reshape(-1, nc, width // nc), c, 1)
    for axis, size, bits in (("z", nz, 1), ("z", nz, 2), ("z", nz, 4), ("y", ny, 1), ("y", ny, 2), ("xh", nh, 1)):
        near_half = jnp.concatenate([near_half, swap(near_half, axis, size, bits)], axis=0)
    far_half = swap(near_half, "c", nc, 1)
    hidden = jnp.concatenate(
        [jnp.where(c == 0, near_half, far_half), jnp.where(c == 0, far_half, near_half)], axis=1
    )

    place = jnp.stack([y, xh]).astype(jnp.int32)
    own = product(True, rows, place, tokens_in, other_tokens, *cots[0])
    place = jnp.stack([y, jnp.where(xl == 0, xh, 1 - xh)]).astype(jnp.int32)
    oth = product(False, rows, place, tokens_in, other_tokens, *cots[1])
    own_y, (own_x0, own_x2a, own_x2b) = own[:4], own[4:]
    oth_y, (oth_x1, oth_x3) = oth[:4], oth[4:]

    up = shift(own_y[2], "y", ny, 1)
    down = shift(own_y[3], "y", ny, -1)
    far = shift(oth_y[2], "y", ny, -1)
    ups = shift(jnp.stack([add(own_y[1], up), oth_y[1]]), "y", ny, 1)
    downs = shift(add(oth_y[3], far), "y", ny, -1)
    after_y = (
        (own_y[0].astype(F32) + ups[0].astype(F32) + down.astype(F32)).astype(BF16),
        (oth_y[0].astype(F32) + ups[1].astype(F32) + downs.astype(F32)).astype(BF16),
    )
    after_y = [a.reshape(nz, nh, rows, part) for a in after_y]

    half = own_x2a.shape[0]
    up = shift(own_x2a, X, nx, 1)
    down = shift(own_x2b, X, nx, -1)
    ups = shift(jnp.concatenate([add(oth_x1[:half], up), oth_x1[half:]]), X, nx, 1)
    downs = shift(jnp.concatenate([oth_x3[:half], add(oth_x3[half:], down)]), X, nx, -1)
    after_x = (own_x0.astype(F32) + ups.astype(F32) + downs.astype(F32)).astype(BF16)
    after_x = after_x.reshape(ny, nz, rows, part)

    def to_x(k):
        return pick(after_y[k % 2], ((x + k) % nx) // nl, 1)

    first = to_x(0).astype(F32)
    second = after_x[0].astype(F32)
    for k in (2, 1, 3):
        first += shift(to_x(k), X, nx, k).astype(F32)
        second += shift(after_x[k], "y", ny, k).astype(F32)
    both = jnp.concatenate([first.astype(BF16), second.astype(BF16)], axis=2)

    def scores(values):
        return lax.dot_general(
            hidden, values, (((1,), (1,)), ((), ())), preferred_element_type=F32
        ).astype(BF16)

    near_scores, far_scores = scores(tokens_in), scores(other_tokens)

    def share(pair):
        return -factor * (
            jnp.dot(near_scores, pair[0], preferred_element_type=F32)
            + jnp.dot(far_scores, pair[1], preferred_element_type=F32)
        )

    at = ((y * nz + z) * nh + xh) * rows
    old = jnp.dot(
        lax.dynamic_slice_in_dim(hidden, at, rows, 1), weight, preferred_element_type=F32
    )
    fresh = share(cots[0]) + old
    fresh = fresh + swap(share(cots[1]).astype(BF16), "xl", nl, 1).astype(F32)
    for axis, size, bits in (("xh", nh, 1), ("y", ny, 2), ("y", ny, 1)):
        split = fresh.shape[0] // 2
        fresh = fresh[:split] + swap(fresh[split:].astype(BF16), axis, size, bits).astype(F32)
    fresh = fresh.astype(BF16).reshape(nz, -1, columns)

    joined = [jnp.concatenate([pick(both, z ^ k), fresh[k]], axis=0) for k in range(nz)]
    parts = joined[:1] + [swap(joined[k], "z", nz, k) for k in range(1, nz)]

    heads = KVH // (nl * nc)
    count = queries.shape[0]
    query = queries.reshape(count, heads, -1, HD)
    group = query.shape[2]
    query = jnp.pad(query, ((0, 0), (0, 0), (0, 8 - group), (0, 0)))
    past = attend_past(query, cache, lengths)
    new_weight, attention = pl.pallas_call(
        functools.partial(finish_kernel, factor, rows),
        in_specs=[VMEM] * (5 + nz),
        out_specs=[VMEM] * 2,
        out_shape=[
            jax.ShapeDtypeStruct(weight.shape, BF16),
            jax.ShapeDtypeStruct(query.shape, BF16),
        ],
        name="finish",
    )(weight, query, *past, *parts)
    return (new_weight, attention[:, :, :group].reshape(count, -1))


def solution(mesh):
    names = ("y", "z", "xh", "xl", "c")
    fine = Mesh(np.asarray(mesh.devices).reshape(4, 8, 2, 2, 2), names)
    fsdp, tp = names[:3], names[3:]
    in_specs = (
        P(names, None),
        P(fsdp, tp),
        P(fsdp, tp),
        P(fsdp, None),
        P(fsdp, tp),
        P(fsdp, None, tp),
        P(fsdp),
    )
    out_specs = (P(fsdp, tp), P(fsdp, tp))
    return jax.shard_map(local, mesh=fine, in_specs=in_specs, out_specs=out_specs, check_vma=False)
```

```python
import functools
import math

import jax
import jax.numpy as jnp
import numpy as np
from jax import lax
from jax.experimental import pallas as pl
from jax.experimental.pallas import tpu as pltpu
from jax.sharding import Mesh
from jax.sharding import PartitionSpec as P

KVH = 8
HD = 128
F32 = jnp.float32
BF16 = jnp.bfloat16
X = ("xh", "xl")
VMEM = pl.BlockSpec(memory_space=pltpu.VMEM)


def shift(value, axis, size, by):
    return lax.ppermute(value, axis, [(i, (i + by) % size) for i in range(size)])


def swap(value, axis, size, bits):
    return lax.ppermute(value, axis, [(i, i ^ bits) for i in range(size)])


def pick(array, index, axis=0):
    return lax.dynamic_index_in_dim(array, index, axis, keepdims=False)


def add(a, b):
    return (a.astype(F32) + b.astype(F32)).astype(BF16)


def product_kernel(rows, place, a_ref, b_ref, ca_ref, cb_ref, *outs):
    by_y, near, far = outs[:4], outs[4:6], outs[6:]
    turn, step = pl.program_id(0), pl.program_id(1)
    values = jnp.concatenate([a_ref[...], b_ref[...]], axis=0)
    cots = jnp.concatenate([ca_ref[...], cb_ref[...]], axis=0)
    total = lax.dot_general(
        values, cots, (((0,), (0,)), ((), ())), preferred_element_type=F32
    ).astype(BF16)
    part = total.shape[1] // 2
    pieces = total.shape[0] // (2 * rows)
    for k in range(4):

        @pl.when(turn == k)
        def _(k=k):
            for i in range(2 * pieces):
                here = slice(i // 2 * rows, (i // 2 + 1) * rows)
                by_y[k][i % 2, here, :] = total[i * rows : (i + 1) * rows, :part]

    for flip in (0, 1):
        for half in (0, 1):

            @pl.when((place[1] == flip) & (step == half))
            def _(flip=flip, half=half):
                for i in range(2 * pieces):
                    out = (near if i % 2 == flip else far)[half]
                    here = slice(i // 2 * rows, (i // 2 + 1) * rows)
                    out[0, here, :] = total[i * rows : (i + 1) * rows, part:]


def product(rows, place, own, other, own_cot, other_cot):
    tokens, width = own.shape
    columns = own_cot.shape[1]
    part = columns // 2
    steps = 2
    tall = width // (4 * steps)

    def of_turn(k):
        return lambda t, s, place: (0, jnp.clip((t - k) * steps + s, 0, steps - 1), 0)

    token_spec = pl.BlockSpec((tokens, tall), lambda t, s, place: (0, ((place[0] + t) % 4) * steps + s))
    whole = pl.BlockSpec((tokens, columns), lambda t, s, place: (0, 0))
    y_specs = [pl.BlockSpec((2, tall // 2, part), of_turn(k)) for k in range(4)]
    y_shapes = [jax.ShapeDtypeStruct((2, width // 8, part), BF16)] * 4
    x_spec = pl.BlockSpec((1, tall // 2, part), lambda t, s, place: ((place[0] + t) % 4, 0, 0))
    x_shape = jax.ShapeDtypeStruct((4, tall // 2, part), BF16)
    return pl.pallas_call(
        functools.partial(product_kernel, rows),
        grid_spec=pltpu.PrefetchScalarGridSpec(
            num_scalar_prefetch=1,
            grid=(4, steps),
            in_specs=[token_spec, token_spec, whole, whole],
            out_specs=y_specs + [x_spec] * 4,
        ),
        out_shape=y_shapes + [x_shape] * 4,
        compiler_params=pltpu.CompilerParams(vmem_limit_bytes=24 << 20),
        cost_estimate=pl.CostEstimate(
            flops=4 * tokens * width * columns, bytes_accessed=6 * tokens * width, transcendentals=0
        ),
        name="product",
    )(place, own, other, own_cot, other_cot)


def past_kernel(heads, lengths, query_ref, cache_ref, sum_ref, top_ref, mass_ref):
    span = cache_ref.shape[1]
    live = lax.broadcasted_iota(jnp.int32, (8, span), 1) < lengths[pl.program_id(0)]
    for j in range(heads):
        keys = cache_ref[0, :, 2 * j * HD : (2 * j + 1) * HD]
        values = cache_ref[0, :, (2 * j + 1) * HD : (2 * j + 2) * HD]
        scores = lax.dot_general(
            query_ref[0, j], keys, (((1,), (1,)), ((), ())), preferred_element_type=F32
        ) / math.sqrt(HD)
        scores = jnp.where(live, scores, jnp.float32(-1e30))
        top = jnp.max(scores, axis=1, keepdims=True)
        weights = jnp.exp(scores - top)
        mass = jnp.sum(weights, axis=1, keepdims=True)
        sum_ref[0, j] = jnp.dot(weights.astype(BF16), values, preferred_element_type=F32)
        top_ref[0, j] = jnp.broadcast_to(top, (8, HD))
        mass_ref[0, j] = jnp.broadcast_to(mass, (8, HD))


def attend_past(query, cache, lengths):
    rows, heads = query.shape[:2]
    span, columns = cache.shape[1:]
    small = pl.BlockSpec((1, heads, 8, HD), lambda r, lengths: (r, 0, 0, 0))
    shape = jax.ShapeDtypeStruct((rows, heads, 8, HD), F32)
    return pl.pallas_call(
        functools.partial(past_kernel, heads),
        grid_spec=pltpu.PrefetchScalarGridSpec(
            num_scalar_prefetch=1,
            grid=(rows,),
            in_specs=[small, pl.BlockSpec((1, span, columns), lambda r, lengths: (r, 0, 0))],
            out_specs=[small] * 3,
        ),
        out_shape=[shape] * 3,
        compiler_params=pltpu.CompilerParams(vmem_limit_bytes=24 << 20),
        cost_estimate=pl.CostEstimate(
            flops=32 * rows * span * columns,
            bytes_accessed=2 * rows * span * columns,
            transcendentals=8 * rows * heads * span,
        ),
        name="past",
    )(lengths, query, cache)


def finish_kernel(
    factor, weight_ref, query_ref, sum_ref, top_ref, mass_ref, parts_ref, weight_out, attention_out
):
    rows = weight_ref.shape[0]
    total = parts_ref[0].astype(F32)
    for k in range(1, parts_ref.shape[0]):
        total += parts_ref[k].astype(F32)
    weight_out[...] = (weight_ref[...].astype(F32) - factor * total[:rows]).astype(BF16)
    fresh = total[rows:].astype(BF16).astype(F32)
    for r in range(query_ref.shape[0]):
        for j in range(query_ref.shape[1]):
            key = fresh[r : r + 1, 2 * j * HD : (2 * j + 1) * HD]
            value = fresh[r : r + 1, (2 * j + 1) * HD : (2 * j + 2) * HD]
            newest = jnp.sum(query_ref[r, j].astype(F32) * key, axis=1, keepdims=True) / math.sqrt(HD)
            old = top_ref[r, j]
            top = jnp.maximum(old, newest)
            past = jnp.exp(old - top)
            new = jnp.exp(newest - top)
            mixed = (sum_ref[r, j] * past + new * value) / (mass_ref[r, j] * past + new)
            attention_out[r, j] = mixed.astype(BF16)


def local(tokens_in, cotangent, weight, hidden_rows, queries, cache, lengths):
    y, z, xh, xl, c = (lax.axis_index(name) for name in ("y", "z", "xh", "xl", "c"))
    ny, nz, nh, nl, nc = (lax.axis_size(name) for name in ("y", "z", "xh", "xl", "c"))
    x = xh * nl + xl
    nx = nh * nl
    tokens, width = tokens_in.shape
    columns = cotangent.shape[1]
    part = columns // 2
    rows = weight.shape[0]
    factor = 0.01 / math.sqrt(tokens * nc * nl * nh * ny * nz)

    heads = KVH // (nl * nc)
    count = queries.shape[0]
    query = queries.reshape(count, heads, -1, HD)
    group = query.shape[2]
    query = jnp.pad(query, ((0, 0), (0, 0), (0, 8 - group), (0, 0)))

    other_tokens = swap(tokens_in, "c", nc, 1)
    blocks = cotangent.reshape(nl, nc, tokens, columns)
    mine = pick(blocks, xl)
    got = swap(pick(blocks, 1 - xl), "xl", nl, 1)
    past = attend_past(query, cache, lengths)
    other_tokens, past = lax.optimization_barrier((other_tokens, past))

    place = jnp.stack([y, xh]).astype(jnp.int32)
    own = product(rows, place, tokens_in, other_tokens, pick(mine, c), pick(mine, 1 - c))
    own_y, (own_x0a, own_x0b, own_x2a, own_x2b) = own[:4], own[4:]
    up = shift(own_y[2], "y", ny, 1)
    down = shift(own_y[3], "y", ny, -1)
    up_x = shift(own_x2a, X, nx, 1)
    down_x = shift(own_x2b, X, nx, -1)

    got, up, down, up_x, down_x = lax.optimization_barrier((got, up, down, up_x, down_x))
    place = jnp.stack([y, jnp.where(xl == 0, xh, 1 - xh)]).astype(jnp.int32)
    oth = product(rows, place, tokens_in, other_tokens, pick(got, c), pick(got, 1 - c))
    oth_y, (oth_x1a, oth_x1b, oth_x3a, oth_x3b) = oth[:4], oth[4:]
    far = shift(oth_y[2], "y", ny, -1)

    far, hidden_rows = lax.optimization_barrier((far, hidden_rows))
    held = hidden_rows.reshape(count, ny, nz, nh, rows).transpose(1, 3, 0, 2, 4)
    held = jnp.broadcast_to(
        held.reshape(ny, 1, nh, count, nz * rows), (ny, nz, nh, count, nz * rows)
    )
    held = lax.all_to_all(
        held.reshape(-1, count, nz * rows), ("y", "z", "xh"), 0, 0, tiled=True
    )
    held = held.reshape(ny, nz, nh, count, nz * rows).transpose(0, 2, 1, 3, 4).reshape(-1, nz * rows)

    ups = shift(jnp.stack([add(own_y[1], up), oth_y[1]]), "y", ny, 1)
    downs = shift(add(oth_y[3], far), "y", ny, -1)
    own_sum = (own_y[0].astype(F32) + ups[0].astype(F32) + down.astype(F32)).astype(BF16)
    oth_sum = (oth_y[0].astype(F32) + ups[1].astype(F32) + downs.astype(F32)).astype(BF16)
    by_x = jnp.stack(
        [jnp.where(xl == 0, own_sum, oth_sum), jnp.where(xl == 0, oth_sum, own_sum)], axis=1
    ).reshape(nx, nz * rows, part)
    first = lax.all_to_all(by_x, X, 0, 0, tiled=True)

    ups = shift(jnp.stack([add(oth_x1a, up_x), oth_x1b], axis=1), X, nx, 1)
    downs = shift(jnp.stack([oth_x3a, add(oth_x3b, down_x)], axis=1), X, nx, -1)
    by_y = (
        jnp.stack([own_x0a, own_x0b], axis=1).astype(F32) + ups.astype(F32) + downs.astype(F32)
    ).astype(BF16)
    by_y = by_y.reshape(ny, nz * rows, part)
    second = pick(by_y, y).astype(F32)
    for k in (2, 1, 3):
        second += shift(pick(by_y, (y + k) % ny), "y", ny, k).astype(F32)
    first = jnp.sum(first.astype(F32), axis=0)
    both = jnp.concatenate([first.astype(BF16), second.astype(BF16)], axis=1)
    both = both.reshape(nz, rows, columns)

    here = (lax.broadcasted_iota(jnp.int32, (nz, 1, 1), 0) == z).astype(F32)
    update = here * weight.astype(F32) - factor * both.astype(F32)
    update = update.astype(BF16).reshape(nz * rows, columns)
    fresh = jnp.dot(held, update, preferred_element_type=F32).astype(BF16)
    fresh = lax.all_to_all(
        fresh.reshape(ny * nh, nz * count, columns), ("y", "xh"), 0, 0, tiled=True
    )
    fresh = jnp.sum(fresh.astype(F32), axis=0).astype(BF16).reshape(nz, count, columns)
    parts = lax.all_to_all(jnp.concatenate([both, fresh], axis=1), "z", 0, 0, tiled=True)

    new_weight, attention = pl.pallas_call(
        functools.partial(finish_kernel, factor),
        in_specs=[VMEM] * 6,
        out_specs=[VMEM] * 2,
        out_shape=[
            jax.ShapeDtypeStruct(weight.shape, BF16),
            jax.ShapeDtypeStruct(query.shape, BF16),
        ],
        name="finish",
    )(weight, query, *past, parts)
    return (new_weight, attention[:, :, :group].reshape(count, -1))


def solution(mesh):
    names = ("y", "z", "xh", "xl", "c")
    fine = Mesh(np.asarray(mesh.devices).reshape(4, 8, 2, 2, 2), names)
    fsdp, tp = names[:3], names[3:]
    in_specs = (
        P(names, None),
        P(fsdp, tp),
        P(fsdp, tp),
        P(fsdp, None),
        P(fsdp, tp),
        P(fsdp, None, tp),
        P(fsdp),
    )
    out_specs = (P(fsdp, tp), P(fsdp, tp))
    return jax.shard_map(local, mesh=fine, in_specs=in_specs, out_specs=out_specs, check_vma=False)
```

```python
import functools
import math

import jax
import jax.numpy as jnp
import numpy as np
from jax import lax
from jax.experimental import pallas as pl
from jax.experimental.pallas import tpu as pltpu
from jax.sharding import Mesh
from jax.sharding import PartitionSpec as P

KVH = 8
HD = 128
F32 = jnp.float32
BF16 = jnp.bfloat16
X = ("xh", "xl")
VMEM = pl.BlockSpec(memory_space=pltpu.VMEM)


def shift(value, axis, size, by):
    return lax.ppermute(value, axis, [(i, (i + by) % size) for i in range(size)])


def swap(value, axis, size, bits):
    return lax.ppermute(value, axis, [(i, i ^ bits) for i in range(size)])


def pick(array, index, axis=0):
    return lax.dynamic_index_in_dim(array, index, axis, keepdims=False)


def add(a, b):
    return (a.astype(F32) + b.astype(F32)).astype(BF16)


def product_kernel(rows, place, a_ref, b_ref, ca_ref, cb_ref, *outs):
    by_y, near, far = outs[:4], outs[4:6], outs[6:]
    turn = pl.program_id(0)
    values = jnp.concatenate([a_ref[...], b_ref[...]], axis=0)
    cots = jnp.concatenate([ca_ref[...], cb_ref[...]], axis=0)
    total = lax.dot_general(
        values, cots, (((0,), (0,)), ((), ())), preferred_element_type=F32
    ).astype(BF16)
    part = total.shape[1] // 2
    pieces = total.shape[0] // rows
    for k in range(4):

        @pl.when(turn == k)
        def _(k=k):
            for i in range(pieces):
                here = slice(i // 2 * rows, (i // 2 + 1) * rows)
                by_y[k][i % 2, here, :] = total[i * rows : (i + 1) * rows, :part]

    for flip in (0, 1):

        @pl.when(place[1] == flip)
        def _(flip=flip):
            for i in range(pieces):
                half, j = divmod(i // 2, pieces // 4)
                out = (near if i % 2 == flip else far)[half]
                out[0, j * rows : (j + 1) * rows, :] = total[i * rows : (i + 1) * rows, part:]


def product(rows, place, own, other, cots):
    tokens, width = own.shape
    columns = cots.shape[2]
    part = columns // 2
    tall = width // 4
    token_spec = pl.BlockSpec((tokens, tall), lambda t, place: (0, (place[0] + t) % 4))
    first_cot = pl.BlockSpec((None, tokens, columns), lambda t, place: (place[2], 0, 0))
    second_cot = pl.BlockSpec((None, tokens, columns), lambda t, place: (place[2] ^ 1, 0, 0))
    y_spec = pl.BlockSpec((2, tall // 2, part), lambda t, place: (0, 0, 0))
    y_shape = jax.ShapeDtypeStruct((2, tall // 2, part), BF16)
    x_spec = pl.BlockSpec((1, tall // 4, part), lambda t, place: ((place[0] + t) % 4, 0, 0))
    x_shape = jax.ShapeDtypeStruct((4, tall // 4, part), BF16)
    return pl.pallas_call(
        functools.partial(product_kernel, rows),
        grid_spec=pltpu.PrefetchScalarGridSpec(
            num_scalar_prefetch=1,
            grid=(4,),
            in_specs=[token_spec, token_spec, first_cot, second_cot],
            out_specs=[y_spec] * 4 + [x_spec] * 4,
        ),
        out_shape=[y_shape] * 4 + [x_shape] * 4,
        compiler_params=pltpu.CompilerParams(vmem_limit_bytes=32 << 20),
        cost_estimate=pl.CostEstimate(
            flops=4 * tokens * width * columns, bytes_accessed=6 * tokens * width, transcendentals=0
        ),
        name="product",
    )(place, own, other, cots, cots)


def past_kernel(heads, lengths, query_ref, cache_ref, sum_ref, top_ref, mass_ref):
    span = cache_ref.shape[1]
    live = lax.broadcasted_iota(jnp.int32, (8, span), 1) < lengths[pl.program_id(0)]
    for j in range(heads):
        keys = cache_ref[0, :, 2 * j * HD : (2 * j + 1) * HD]
        values = cache_ref[0, :, (2 * j + 1) * HD : (2 * j + 2) * HD]
        scores = lax.dot_general(
            query_ref[0, j], keys, (((1,), (1,)), ((), ())), preferred_element_type=F32
        ) / math.sqrt(HD)
        scores = jnp.where(live, scores, jnp.float32(-1e30))
        top = jnp.max(scores, axis=1, keepdims=True)
        weights = jnp.exp(scores - top)
        mass = jnp.sum(weights, axis=1, keepdims=True)
        sum_ref[0, j] = jnp.dot(weights.astype(BF16), values, preferred_element_type=F32)
        top_ref[0, j] = jnp.broadcast_to(top, (8, HD))
        mass_ref[0, j] = jnp.broadcast_to(mass, (8, HD))


def attend_past(query, cache, lengths):
    rows, heads = query.shape[:2]
    span, columns = cache.shape[1:]
    small = pl.BlockSpec((1, heads, 8, HD), lambda r, lengths: (r, 0, 0, 0))
    shape = jax.ShapeDtypeStruct((rows, heads, 8, HD), F32)
    return pl.pallas_call(
        functools.partial(past_kernel, heads),
        grid_spec=pltpu.PrefetchScalarGridSpec(
            num_scalar_prefetch=1,
            grid=(rows,),
            in_specs=[small, pl.BlockSpec((1, span, columns), lambda r, lengths: (r, 0, 0))],
            out_specs=[small] * 3,
        ),
        out_shape=[shape] * 3,
        compiler_params=pltpu.CompilerParams(vmem_limit_bytes=24 << 20),
        cost_estimate=pl.CostEstimate(
            flops=32 * rows * span * columns,
            bytes_accessed=2 * rows * span * columns,
            transcendentals=8 * rows * heads * span,
        ),
        name="past",
    )(lengths, query, cache)


def finish_kernel(
    factor, weight_ref, query_ref, sum_ref, top_ref, mass_ref, parts_ref, weight_out, attention_out
):
    rows = weight_ref.shape[0]
    total = parts_ref[0].astype(F32)
    for k in range(1, parts_ref.shape[0]):
        total += parts_ref[k].astype(F32)
    weight_out[...] = (weight_ref[...].astype(F32) - factor * total[:rows]).astype(BF16)
    fresh = total[rows:].astype(BF16).astype(F32)
    heads, group = sum_ref.shape[:2]
    for j in range(heads):
        key = fresh[:, 2 * j * HD : (2 * j + 1) * HD]
        value = fresh[:, (2 * j + 1) * HD : (2 * j + 2) * HD]
        for g in range(group):
            here = slice((j * group + g) * HD, (j * group + g + 1) * HD)
            query = query_ref[:, here].astype(F32)
            newest = jnp.sum(query * key, axis=1, keepdims=True) / math.sqrt(HD)
            old = top_ref[j, g]
            top = jnp.maximum(old, newest)
            past = jnp.exp(old - top)
            new = jnp.exp(newest - top)
            mixed = (sum_ref[j, g] * past + new * value) / (mass_ref[j, g] * past + new)
            attention_out[:, here] = mixed.astype(BF16)


def local(tokens_in, cotangent, weight, hidden_rows, queries, cache, lengths):
    y, z, xh, xl, c = (lax.axis_index(name) for name in ("y", "z", "xh", "xl", "c"))
    ny, nz, nh, nl, nc = (lax.axis_size(name) for name in ("y", "z", "xh", "xl", "c"))
    x = xh * nl + xl
    nx = nh * nl
    tokens, width = tokens_in.shape
    columns = cotangent.shape[1]
    part = columns // 2
    rows = weight.shape[0]
    factor = 0.01 / math.sqrt(tokens * nc * nl * nh * ny * nz)

    heads = KVH // (nl * nc)
    count = queries.shape[0]
    query = queries.reshape(count, heads, -1, HD)
    group = query.shape[2]
    query = jnp.pad(query, ((0, 0), (0, 0), (0, 8 - group), (0, 0)))

    other_tokens = swap(tokens_in, "c", nc, 1)
    blocks = cotangent.reshape(nl, nc, tokens, columns)
    got = swap(pick(blocks, 1 - xl), "xl", nl, 1)

    place = jnp.stack([y, xh, xl * nc + c]).astype(jnp.int32)
    own = product(
        rows, place, tokens_in, other_tokens, cotangent.reshape(nl * nc, tokens, columns)
    )
    own_y, (own_x0a, own_x0b, own_x2a, own_x2b) = own[:4], own[4:]
    up = shift(own_y[2], "y", ny, 1)
    down = shift(own_y[3], "y", ny, -1)
    up_x = shift(own_x2a, X, nx, 1)
    down_x = shift(own_x2b, X, nx, -1)

    place = jnp.stack([y, jnp.where(xl == 0, xh, 1 - xh), c]).astype(jnp.int32)
    oth = product(rows, place, tokens_in, other_tokens, got)
    oth_y, (oth_x1a, oth_x1b, oth_x3a, oth_x3b) = oth[:4], oth[4:]
    oth_y2, up, down, up_x, down_x, query = lax.optimization_barrier(
        (oth_y[2], up, down, up_x, down_x, query)
    )
    far = shift(oth_y2, "y", ny, -1)
    past = attend_past(query, cache, lengths)

    far, hidden_rows = lax.optimization_barrier((far, hidden_rows))
    held = hidden_rows.reshape(count, ny, nz, nh, rows).transpose(1, 3, 0, 2, 4)
    held = jnp.broadcast_to(
        held.reshape(ny, 1, nh, count, nz * rows), (ny, nz, nh, count, nz * rows)
    )
    held = lax.all_to_all(
        held.reshape(-1, count, nz * rows), ("y", "z", "xh"), 0, 0, tiled=True
    )
    held = held.reshape(ny, nz, nh, count, nz * rows).transpose(0, 2, 1, 3, 4).reshape(-1, nz * rows)

    oth_up = shift(oth_y[1], "y", ny, 1)
    own_up = shift(add(own_y[1], up), "y", ny, 1)
    oth_down = shift(add(oth_y[3], far), "y", ny, -1)
    up_b = shift(oth_x1b, X, nx, 1)
    down_a = shift(oth_x3a, X, nx, -1)
    up_a = shift(add(oth_x1a, up_x), X, nx, 1)
    down_b = shift(add(oth_x3b, down_x), X, nx, -1)

    def after_y(k):
        index = ((x + k) % nx) // nl
        terms = (oth_y[0], oth_up, oth_down) if k % 2 else (own_y[0], own_up, down)
        return sum(pick(term, index).astype(F32) for term in terms)

    by_y = (
        jnp.stack([own_x0a, own_x0b], axis=1).astype(F32)
        + jnp.stack([up_a, up_b], axis=1).astype(F32)
        + jnp.stack([down_a, down_b], axis=1).astype(F32)
    ).astype(BF16)
    by_y = by_y.reshape(ny, nz * rows, part)
    first, second = after_y(0), pick(by_y, y).astype(F32)
    for k in (2, 1, 3):
        first += shift(after_y(k).astype(BF16), X, nx, k).astype(F32)
        second += shift(pick(by_y, (y + k) % ny), "y", ny, k).astype(F32)
    both = jnp.concatenate([first.astype(BF16), second.astype(BF16)], axis=1)
    both = both.reshape(nz, rows, columns)

    here = (lax.broadcasted_iota(jnp.int32, (nz, 1, 1), 0) == z).astype(F32)
    update = here * weight.astype(F32) - factor * both.astype(F32)
    update = update.astype(BF16).reshape(nz * rows, columns)
    fresh = jnp.dot(held, update, preferred_element_type=F32).astype(BF16)
    fresh = lax.all_to_all(
        fresh.reshape(ny * nh, nz * count, columns), ("y", "xh"), 0, 0, tiled=True
    )
    fresh = jnp.sum(fresh.astype(F32), axis=0).astype(BF16).reshape(nz, count, columns)
    parts = lax.all_to_all(jnp.concatenate([both, fresh], axis=1), "z", 0, 0, tiled=True)

    past = [values[:, :, :group].transpose(1, 2, 0, 3) for values in past]
    return pl.pallas_call(
        functools.partial(finish_kernel, factor),
        in_specs=[VMEM] * 6,
        out_specs=[VMEM] * 2,
        out_shape=[
            jax.ShapeDtypeStruct(weight.shape, BF16),
            jax.ShapeDtypeStruct(queries.shape, BF16),
        ],
        name="finish",
    )(weight, queries, *past, parts)


def solution(mesh):
    names = ("y", "z", "xh", "xl", "c")
    fine = Mesh(np.asarray(mesh.devices).reshape(4, 8, 2, 2, 2), names)
    fsdp, tp = names[:3], names[3:]
    in_specs = (
        P(names, None),
        P(fsdp, tp),
        P(fsdp, tp),
        P(fsdp, None),
        P(fsdp, tp),
        P(fsdp, None, tp),
        P(fsdp),
    )
    out_specs = (P(fsdp, tp), P(fsdp, tp))
    return jax.shard_map(local, mesh=fine, in_specs=in_specs, out_specs=out_specs, check_vma=False)
```

```python
import functools
import math

import jax
import jax.numpy as jnp
import numpy as np
from jax import lax
from jax.experimental import pallas as pl
from jax.experimental.pallas import tpu as pltpu
from jax.sharding import Mesh
from jax.sharding import PartitionSpec as P

KVH = 8
HD = 128
F32 = jnp.float32
BF16 = jnp.bfloat16
X = ("xh", "xl")
VMEM = pl.BlockSpec(memory_space=pltpu.VMEM)


def shift(value, axis, size, by):
    return lax.ppermute(value, axis, [(i, (i + by) % size) for i in range(size)])


def swap(value, axis, size, bits):
    return lax.ppermute(value, axis, [(i, i ^ bits) for i in range(size)])


def pick(array, index, axis=0):
    return lax.dynamic_index_in_dim(array, index, axis, keepdims=False)


def add(a, b):
    return (a.astype(F32) + b.astype(F32)).astype(BF16)


def product_kernel(rows, place, a_ref, b_ref, ca_ref, cb_ref, *outs):
    by_y, near, far = outs[:4], outs[4:6], outs[6:]
    turn = pl.program_id(0)
    values = jnp.concatenate([a_ref[...], b_ref[...]], axis=0)
    cots = jnp.concatenate([ca_ref[...], cb_ref[...]], axis=0)
    total = lax.dot_general(
        values, cots, (((0,), (0,)), ((), ())), preferred_element_type=F32
    ).astype(BF16)
    part = total.shape[1] // 2
    pieces = total.shape[0] // rows
    for k in range(4):

        @pl.when(turn == k)
        def _(k=k):
            for i in range(pieces):
                here = slice(i // 2 * rows, (i // 2 + 1) * rows)
                by_y[k][i % 2, here, :] = total[i * rows : (i + 1) * rows, :part]

    for flip in (0, 1):

        @pl.when(place[1] == flip)
        def _(flip=flip):
            for i in range(pieces):
                half, j = divmod(i // 2, pieces // 4)
                out = (near if i % 2 == flip else far)[half]
                out[0, j * rows : (j + 1) * rows, :] = total[i * rows : (i + 1) * rows, part:]


def product(rows, place, own, other, cots):
    tokens, width = own.shape
    columns = cots.shape[2]
    part = columns // 2
    tall = width // 4
    token_spec = pl.BlockSpec((tokens, tall), lambda t, place: (0, (place[0] + t) % 4))
    first_cot = pl.BlockSpec((None, tokens, columns), lambda t, place: (place[2], 0, 0))
    second_cot = pl.BlockSpec((None, tokens, columns), lambda t, place: (place[2] ^ 1, 0, 0))
    y_spec = pl.BlockSpec((2, tall // 2, part), lambda t, place: (0, 0, 0))
    y_shape = jax.ShapeDtypeStruct((2, tall // 2, part), BF16)
    x_spec = pl.BlockSpec((1, tall // 4, part), lambda t, place: ((place[0] + t) % 4, 0, 0))
    x_shape = jax.ShapeDtypeStruct((4, tall // 4, part), BF16)
    return pl.pallas_call(
        functools.partial(product_kernel, rows),
        grid_spec=pltpu.PrefetchScalarGridSpec(
            num_scalar_prefetch=1,
            grid=(4,),
            in_specs=[token_spec, token_spec, first_cot, second_cot],
            out_specs=[y_spec] * 4 + [x_spec] * 4,
        ),
        out_shape=[y_shape] * 4 + [x_shape] * 4,
        compiler_params=pltpu.CompilerParams(vmem_limit_bytes=32 << 20),
        cost_estimate=pl.CostEstimate(
            flops=4 * tokens * width * columns, bytes_accessed=6 * tokens * width, transcendentals=0
        ),
        name="product",
    )(place, own, other, cots, cots)


def past_kernel(heads, lengths, query_ref, cache_ref, sum_ref, top_ref, mass_ref):
    span = cache_ref.shape[1]
    live = lax.broadcasted_iota(jnp.int32, (8, span), 1) < lengths[pl.program_id(0)]
    for j in range(heads):
        keys = cache_ref[0, :, 2 * j * HD : (2 * j + 1) * HD]
        values = cache_ref[0, :, (2 * j + 1) * HD : (2 * j + 2) * HD]
        scores = lax.dot_general(
            query_ref[0, j], keys, (((1,), (1,)), ((), ())), preferred_element_type=F32
        ) / math.sqrt(HD)
        scores = jnp.where(live, scores, jnp.float32(-1e30))
        top = jnp.max(scores, axis=1, keepdims=True)
        weights = jnp.exp(scores - top)
        mass = jnp.sum(weights, axis=1, keepdims=True)
        sum_ref[0, j] = jnp.dot(weights.astype(BF16), values, preferred_element_type=F32)
        top_ref[0, j] = jnp.broadcast_to(top, (8, HD))
        mass_ref[0, j] = jnp.broadcast_to(mass, (8, HD))


def attend_past(query, cache, lengths):
    rows, heads = query.shape[:2]
    span, columns = cache.shape[1:]
    small = pl.BlockSpec((1, heads, 8, HD), lambda r, lengths: (r, 0, 0, 0))
    shape = jax.ShapeDtypeStruct((rows, heads, 8, HD), F32)
    return pl.pallas_call(
        functools.partial(past_kernel, heads),
        grid_spec=pltpu.PrefetchScalarGridSpec(
            num_scalar_prefetch=1,
            grid=(rows,),
            in_specs=[small, pl.BlockSpec((1, span, columns), lambda r, lengths: (r, 0, 0))],
            out_specs=[small] * 3,
        ),
        out_shape=[shape] * 3,
        compiler_params=pltpu.CompilerParams(vmem_limit_bytes=24 << 20),
        cost_estimate=pl.CostEstimate(
            flops=32 * rows * span * columns,
            bytes_accessed=2 * rows * span * columns,
            transcendentals=8 * rows * heads * span,
        ),
        name="past",
    )(lengths, query, cache)


def finish_kernel(
    factor, weight_ref, query_ref, sum_ref, top_ref, mass_ref, parts_ref, weight_out, attention_out
):
    rows = weight_ref.shape[0]
    total = parts_ref[0].astype(F32)
    for k in range(1, parts_ref.shape[0]):
        total += parts_ref[k].astype(F32)
    weight_out[...] = (weight_ref[...].astype(F32) - factor * total[:rows]).astype(BF16)
    fresh = total[rows:].astype(BF16).astype(F32)
    heads, group = sum_ref.shape[:2]
    for j in range(heads):
        key = fresh[:, 2 * j * HD : (2 * j + 1) * HD]
        value = fresh[:, (2 * j + 1) * HD : (2 * j + 2) * HD]
        for g in range(group):
            here = slice((j * group + g) * HD, (j * group + g + 1) * HD)
            query = query_ref[:, here].astype(F32)
            newest = jnp.sum(query * key, axis=1, keepdims=True) / math.sqrt(HD)
            old = top_ref[j, g]
            top = jnp.maximum(old, newest)
            past = jnp.exp(old - top)
            new = jnp.exp(newest - top)
            mixed = (sum_ref[j, g] * past + new * value) / (mass_ref[j, g] * past + new)
            attention_out[:, here] = mixed.astype(BF16)


def local(tokens_in, cotangent, weight, hidden_rows, queries, cache, lengths):
    y, z, xh, xl, c = (lax.axis_index(name) for name in ("y", "z", "xh", "xl", "c"))
    ny, nz, nh, nl, nc = (lax.axis_size(name) for name in ("y", "z", "xh", "xl", "c"))
    x = xh * nl + xl
    nx = nh * nl
    tokens, width = tokens_in.shape
    columns = cotangent.shape[1]
    part = columns // 2
    rows = weight.shape[0]
    factor = 0.01 / math.sqrt(tokens * nc * nl * nh * ny * nz)

    heads = KVH // (nl * nc)
    count = queries.shape[0]
    query = queries.reshape(count, heads, -1, HD)
    group = query.shape[2]
    query = jnp.pad(query, ((0, 0), (0, 0), (0, 8 - group), (0, 0)))

    other_tokens = swap(tokens_in, "c", nc, 1)
    blocks = cotangent.reshape(nl, nc, tokens, columns)
    got = swap(pick(blocks, 1 - xl), "xl", nl, 1)

    held = hidden_rows.reshape(count, ny, nz, nh, rows).transpose(3, 1, 0, 2, 4)
    held = held.reshape(nh, ny, count, nz * rows)
    ours, theirs = pick(held, xh), swap(pick(held, 1 - xh), "xh", nh, 1)
    held = jnp.concatenate(
        [jnp.where(xh == 0, ours, theirs), jnp.where(xh == 0, theirs, ours)], axis=1
    )

    place = jnp.stack([y, xh, xl * nc + c]).astype(jnp.int32)
    own = product(
        rows, place, tokens_in, other_tokens, cotangent.reshape(nl * nc, tokens, columns)
    )
    own_y, (own_x0a, own_x0b, own_x2a, own_x2b) = own[:4], own[4:]
    up = shift(own_y[2], "y", ny, 1)
    down = shift(own_y[3], "y", ny, -1)
    up_x = shift(own_x2a, X, nx, 1)
    down_x = shift(own_x2b, X, nx, -1)

    place = jnp.stack([y, jnp.where(xl == 0, xh, 1 - xh), c]).astype(jnp.int32)
    oth = product(rows, place, tokens_in, other_tokens, got)
    oth_y, (oth_x1a, oth_x1b, oth_x3a, oth_x3b) = oth[:4], oth[4:]
    oth_y2, up, down, up_x, down_x, query = lax.optimization_barrier(
        (oth_y[2], up, down, up_x, down_x, query)
    )
    far = shift(oth_y2, "y", ny, -1)
    past = attend_past(query, cache, lengths)

    far, held = lax.optimization_barrier((far, held))
    held = jnp.broadcast_to(held[:, None], (ny, nz, *held.shape[1:]))
    held = lax.all_to_all(
        held.reshape(ny * nz, nh * count, nz * rows), ("y", "z"), 0, 0, tiled=True
    ).reshape(-1, nz * rows)

    oth_up = shift(oth_y[1], "y", ny, 1)
    own_up = shift(add(own_y[1], up), "y", ny, 1)
    far, oth_up = lax.optimization_barrier((far, oth_up))
    oth_down = shift(add(oth_y[3], far), "y", ny, -1)
    up_b = shift(oth_x1b, X, nx, 1)
    down_a = shift(oth_x3a, X, nx, -1)
    up_a = shift(add(oth_x1a, up_x), X, nx, 1)
    down_b = shift(add(oth_x3b, down_x), X, nx, -1)

    up_a, up_b, down_a, down_b, own_up = lax.optimization_barrier(
        (up_a, up_b, down_a, down_b, own_up)
    )

    def after_y(k):
        index = ((x + k) % nx) // nl
        terms = (oth_y[0], oth_up, oth_down) if k % 2 else (own_y[0], own_up, down)
        return sum(pick(term, index).astype(F32) for term in terms)

    by_y = (
        jnp.stack([own_x0a, own_x0b], axis=1).astype(F32)
        + jnp.stack([up_a, up_b], axis=1).astype(F32)
        + jnp.stack([down_a, down_b], axis=1).astype(F32)
    ).astype(BF16)
    by_y = by_y.reshape(ny, nz * rows, part)
    first, second = after_y(0), pick(by_y, y).astype(F32)
    for k in (2, 1, 3):
        first += shift(after_y(k).astype(BF16), X, nx, k).astype(F32)
        second += shift(pick(by_y, (y + k) % ny), "y", ny, k).astype(F32)
    both = jnp.concatenate([first.astype(BF16), second.astype(BF16)], axis=1)
    both = both.reshape(nz, rows, columns)

    here = (lax.broadcasted_iota(jnp.int32, (nz, 1, 1), 0) == z).astype(F32)
    update = here * weight.astype(F32) - factor * both.astype(F32)
    update = update.astype(BF16).reshape(nz * rows, columns)
    fresh = jnp.dot(held, update, preferred_element_type=F32).astype(BF16)
    fresh = fresh.reshape(ny, nz, nh, count, columns).transpose(0, 2, 1, 3, 4)
    fresh = lax.all_to_all(
        fresh.reshape(ny * nh, nz * count, columns), ("y", "xh"), 0, 0, tiled=True
    )
    fresh = jnp.sum(fresh.astype(F32), axis=0).astype(BF16).reshape(nz, count, columns)
    parts = lax.all_to_all(jnp.concatenate([both, fresh], axis=1), "z", 0, 0, tiled=True)

    past = [values[:, :, :group].transpose(1, 2, 0, 3) for values in past]
    return pl.pallas_call(
        functools.partial(finish_kernel, factor),
        in_specs=[VMEM] * 6,
        out_specs=[VMEM] * 2,
        out_shape=[
            jax.ShapeDtypeStruct(weight.shape, BF16),
            jax.ShapeDtypeStruct(queries.shape, BF16),
        ],
        name="finish",
    )(weight, queries, *past, parts)


def solution(mesh):
    names = ("y", "z", "xh", "xl", "c")
    fine = Mesh(np.asarray(mesh.devices).reshape(4, 8, 2, 2, 2), names)
    fsdp, tp = names[:3], names[3:]
    in_specs = (
        P(names, None),
        P(fsdp, tp),
        P(fsdp, tp),
        P(fsdp, None),
        P(fsdp, tp),
        P(fsdp, None, tp),
        P(fsdp),
    )
    out_specs = (P(fsdp, tp), P(fsdp, tp))
    return jax.shard_map(local, mesh=fine, in_specs=in_specs, out_specs=out_specs, check_vma=False)
```

```python
import functools
import math

import jax
import jax.numpy as jnp
import numpy as np
from jax import lax
from jax.experimental import pallas as pl
from jax.experimental.pallas import tpu as pltpu
from jax.sharding import Mesh
from jax.sharding import PartitionSpec as P

KVH = 8
HD = 128
F32 = jnp.float32
BF16 = jnp.bfloat16
X = ("xh", "xl")
VMEM = pl.BlockSpec(memory_space=pltpu.VMEM)


def shift(value, axis, size, by):
    return lax.ppermute(value, axis, [(i, (i + by) % size) for i in range(size)])


def swap(value, axis, size, bits):
    return lax.ppermute(value, axis, [(i, i ^ bits) for i in range(size)])


def pick(array, index, axis=0):
    return lax.dynamic_index_in_dim(array, index, axis, keepdims=False)


def add(a, b):
    return (a.astype(F32) + b.astype(F32)).astype(BF16)


def product_kernel(rows, place, a_ref, b_ref, ca_ref, cb_ref, *outs):
    values = jnp.concatenate([a_ref[...], b_ref[...]], axis=0)
    cots = jnp.concatenate([ca_ref[...], cb_ref[...]], axis=0)
    store(rows, place, tokens_by(values, cots).astype(BF16), outs)


def rest_kernel(rows, place, head_ref, b_ref, cb_ref, *outs):
    total = tokens_by(b_ref[...], cb_ref[...]) + head_ref[...].astype(F32)
    store(rows, place, total.astype(BF16), outs)


def head_kernel(place, a_ref, ca_ref, out_ref):
    out_ref[...] = tokens_by(a_ref[...], ca_ref[...]).astype(BF16)


def tokens_by(values, cots):
    return lax.dot_general(values, cots, (((0,), (0,)), ((), ())), preferred_element_type=F32)


def store(rows, place, total, outs):
    by_y, near, far = outs[:4], outs[4:6], outs[6:]
    turn = pl.program_id(0)
    part = total.shape[1] // 2
    pieces = total.shape[0] // rows
    for k in range(4):

        @pl.when(turn == k)
        def _(k=k):
            for i in range(pieces):
                here = slice(i // 2 * rows, (i // 2 + 1) * rows)
                by_y[k][i % 2, here, :] = total[i * rows : (i + 1) * rows, :part]

    for flip in (0, 1):

        @pl.when(place[1] == flip)
        def _(flip=flip):
            for i in range(pieces):
                half, j = divmod(i // 2, pieces // 4)
                out = (near if i % 2 == flip else far)[half]
                out[0, j * rows : (j + 1) * rows, :] = total[i * rows : (i + 1) * rows, part:]


def product(rows, place, own, other, cots, head=None):
    tokens, width = own.shape
    columns = cots.shape[2]
    part = columns // 2
    tall = width // 4
    token_spec = pl.BlockSpec((tokens, tall), lambda t, place: (0, (place[0] + t) % 4))
    first_cot = pl.BlockSpec((None, tokens, columns), lambda t, place: (place[2], 0, 0))
    second_cot = pl.BlockSpec((None, tokens, columns), lambda t, place: (place[2] ^ 1, 0, 0))
    head_spec = pl.BlockSpec((tall, columns), lambda t, place: ((place[0] + t) % 4, 0))
    y_spec = pl.BlockSpec((2, tall // 2, part), lambda t, place: (0, 0, 0))
    y_shape = jax.ShapeDtypeStruct((2, tall // 2, part), BF16)
    x_spec = pl.BlockSpec((1, tall // 4, part), lambda t, place: ((place[0] + t) % 4, 0, 0))
    x_shape = jax.ShapeDtypeStruct((4, tall // 4, part), BF16)
    out_specs, out_shape = [y_spec] * 4 + [x_spec] * 4, [y_shape] * 4 + [x_shape] * 4
    kernel, name, share = functools.partial(product_kernel, rows), "product", 2
    in_specs, args = [token_spec, token_spec, first_cot, second_cot], (own, other, cots, cots)
    if head is not None:
        kernel, name, share = functools.partial(rest_kernel, rows), "rest", 1
        in_specs, args = [head_spec, token_spec, second_cot], (head, other, cots)
    elif other is None:
        kernel, name, share = head_kernel, "head", 1
        in_specs, args = [token_spec, first_cot], (own, cots)
        out_specs, out_shape = head_spec, jax.ShapeDtypeStruct((width, columns), BF16)
    return pl.pallas_call(
        kernel,
        grid_spec=pltpu.PrefetchScalarGridSpec(
            num_scalar_prefetch=1, grid=(4,), in_specs=in_specs, out_specs=out_specs
        ),
        out_shape=out_shape,
        compiler_params=pltpu.CompilerParams(vmem_limit_bytes=32 << 20),
        cost_estimate=pl.CostEstimate(
            flops=2 * share * tokens * width * columns,
            bytes_accessed=6 * tokens * width,
            transcendentals=0,
        ),
        name=name,
    )(place, *args)


def past_kernel(heads, lengths, query_ref, cache_ref, sum_ref, top_ref, mass_ref):
    span = cache_ref.shape[1]
    live = lax.broadcasted_iota(jnp.int32, (8, span), 1) < lengths[pl.program_id(0)]
    for j in range(heads):
        keys = cache_ref[0, :, 2 * j * HD : (2 * j + 1) * HD]
        values = cache_ref[0, :, (2 * j + 1) * HD : (2 * j + 2) * HD]
        scores = lax.dot_general(
            query_ref[0, j], keys, (((1,), (1,)), ((), ())), preferred_element_type=F32
        ) / math.sqrt(HD)
        scores = jnp.where(live, scores, jnp.float32(-1e30))
        top = jnp.max(scores, axis=1, keepdims=True)
        weights = jnp.exp(scores - top)
        mass = jnp.sum(weights, axis=1, keepdims=True)
        sum_ref[0, j] = jnp.dot(weights.astype(BF16), values, preferred_element_type=F32)
        top_ref[0, j] = jnp.broadcast_to(top, (8, HD))
        mass_ref[0, j] = jnp.broadcast_to(mass, (8, HD))


def attend_past(query, cache, lengths):
    rows, heads = query.shape[:2]
    span, columns = cache.shape[1:]
    small = pl.BlockSpec((1, heads, 8, HD), lambda r, lengths: (r, 0, 0, 0))
    shape = jax.ShapeDtypeStruct((rows, heads, 8, HD), F32)
    return pl.pallas_call(
        functools.partial(past_kernel, heads),
        grid_spec=pltpu.PrefetchScalarGridSpec(
            num_scalar_prefetch=1,
            grid=(rows,),
            in_specs=[small, pl.BlockSpec((1, span, columns), lambda r, lengths: (r, 0, 0))],
            out_specs=[small] * 3,
        ),
        out_shape=[shape] * 3,
        compiler_params=pltpu.CompilerParams(vmem_limit_bytes=24 << 20),
        cost_estimate=pl.CostEstimate(
            flops=32 * rows * span * columns,
            bytes_accessed=2 * rows * span * columns,
            transcendentals=8 * rows * heads * span,
        ),
        name="past",
    )(lengths, query, cache)


def finish_kernel(
    factor, weight_ref, query_ref, sum_ref, top_ref, mass_ref, parts_ref, weight_out, attention_out
):
    rows = weight_ref.shape[0]
    total = parts_ref[0].astype(F32)
    for k in range(1, parts_ref.shape[0]):
        total += parts_ref[k].astype(F32)
    weight_out[...] = (weight_ref[...].astype(F32) - factor * total[:rows]).astype(BF16)
    fresh = total[rows:].astype(BF16).astype(F32)
    heads, group = sum_ref.shape[:2]
    for j in range(heads):
        key = fresh[:, 2 * j * HD : (2 * j + 1) * HD]
        value = fresh[:, (2 * j + 1) * HD : (2 * j + 2) * HD]
        for g in range(group):
            here = slice((j * group + g) * HD, (j * group + g + 1) * HD)
            query = query_ref[:, here].astype(F32)
            newest = jnp.sum(query * key, axis=1, keepdims=True) / math.sqrt(HD)
            old = top_ref[j, g]
            top = jnp.maximum(old, newest)
            past = jnp.exp(old - top)
            new = jnp.exp(newest - top)
            mixed = (sum_ref[j, g] * past + new * value) / (mass_ref[j, g] * past + new)
            attention_out[:, here] = mixed.astype(BF16)


def local(tokens_in, cotangent, weight, hidden_rows, queries, cache, lengths):
    y, z, xh, xl, c = (lax.axis_index(name) for name in ("y", "z", "xh", "xl", "c"))
    ny, nz, nh, nl, nc = (lax.axis_size(name) for name in ("y", "z", "xh", "xl", "c"))
    x = xh * nl + xl
    nx = nh * nl
    tokens, width = tokens_in.shape
    columns = cotangent.shape[1]
    part = columns // 2
    rows = weight.shape[0]
    factor = 0.01 / math.sqrt(tokens * nc * nl * nh * ny * nz)

    heads = KVH // (nl * nc)
    count = queries.shape[0]
    query = queries.reshape(count, heads, -1, HD)
    group = query.shape[2]
    query = jnp.pad(query, ((0, 0), (0, 0), (0, 8 - group), (0, 0)))

    other_tokens = swap(tokens_in, "c", nc, 1)
    blocks = cotangent.reshape(nl, nc, tokens, columns)
    got = swap(pick(blocks, 1 - xl), "xl", nl, 1)

    held = hidden_rows.reshape(count, ny, nz, nh, rows).transpose(3, 1, 0, 2, 4)
    held = held.reshape(nh, ny, count, nz * rows)
    ours, theirs = pick(held, xh), swap(pick(held, 1 - xh), "xh", nh, 1)
    held = jnp.concatenate(
        [jnp.where(xh == 0, ours, theirs), jnp.where(xh == 0, theirs, ours)], axis=1
    )

    place = jnp.stack([y, xh, xl * nc + c]).astype(jnp.int32)
    own_cots = cotangent.reshape(nl * nc, tokens, columns)
    head = product(rows, place, tokens_in, None, own_cots)
    own = product(rows, place, tokens_in, other_tokens, own_cots, head)
    own_y, (own_x0a, own_x0b, own_x2a, own_x2b) = own[:4], own[4:]
    up = shift(own_y[2], "y", ny, 1)
    down = shift(own_y[3], "y", ny, -1)
    up_x = shift(own_x2a, X, nx, 1)
    down_x = shift(own_x2b, X, nx, -1)

    place = jnp.stack([y, jnp.where(xl == 0, xh, 1 - xh), c]).astype(jnp.int32)
    oth = product(rows, place, tokens_in, other_tokens, got)
    oth_y, (oth_x1a, oth_x1b, oth_x3a, oth_x3b) = oth[:4], oth[4:]
    oth_y2, up, down, up_x, down_x, query = lax.optimization_barrier(
        (oth_y[2], up, down, up_x, down_x, query)
    )
    far = shift(oth_y2, "y", ny, -1)
    past = attend_past(query, cache, lengths)

    far, held = lax.optimization_barrier((far, held))
    held = jnp.broadcast_to(held[:, None], (ny, nz, *held.shape[1:]))
    held = lax.all_to_all(
        held.reshape(ny * nz, nh * count, nz * rows), ("y", "z"), 0, 0, tiled=True
    ).reshape(-1, nz * rows)

    oth_up = shift(oth_y[1], "y", ny, 1)
    own_up = shift(add(own_y[1], up), "y", ny, 1)
    far, oth_up = lax.optimization_barrier((far, oth_up))
    oth_down = shift(add(oth_y[3], far), "y", ny, -1)
    up_b = shift(oth_x1b, X, nx, 1)
    down_a = shift(oth_x3a, X, nx, -1)
    up_a = shift(add(oth_x1a, up_x), X, nx, 1)
    down_b = shift(add(oth_x3b, down_x), X, nx, -1)

    up_a, up_b, down_a, down_b, own_up = lax.optimization_barrier(
        (up_a, up_b, down_a, down_b, own_up)
    )

    def after_y(k):
        index = ((x + k) % nx) // nl
        terms = (oth_y[0], oth_up, oth_down) if k % 2 else (own_y[0], own_up, down)
        return sum(pick(term, index).astype(F32) for term in terms)

    by_y = (
        jnp.stack([own_x0a, own_x0b], axis=1).astype(F32)
        + jnp.stack([up_a, up_b], axis=1).astype(F32)
        + jnp.stack([down_a, down_b], axis=1).astype(F32)
    ).astype(BF16)
    by_y = by_y.reshape(ny, nz * rows, part)
    first, second = after_y(0), pick(by_y, y).astype(F32)
    for k in (2, 1, 3):
        first += shift(after_y(k).astype(BF16), X, nx, k).astype(F32)
        second += shift(pick(by_y, (y + k) % ny), "y", ny, k).astype(F32)
    both = jnp.concatenate([first.astype(BF16), second.astype(BF16)], axis=1)
    both = both.reshape(nz, rows, columns)

    here = (lax.broadcasted_iota(jnp.int32, (nz, 1, 1), 0) == z).astype(F32)
    update = here * weight.astype(F32) - factor * both.astype(F32)
    update = update.astype(BF16).reshape(nz * rows, columns)
    fresh = jnp.dot(held, update, preferred_element_type=F32).astype(BF16)
    fresh = fresh.reshape(ny, nz, nh, count, columns).transpose(0, 2, 1, 3, 4)
    fresh = lax.all_to_all(
        fresh.reshape(ny * nh, nz * count, columns), ("y", "xh"), 0, 0, tiled=True
    )
    fresh = jnp.sum(fresh.astype(F32), axis=0).astype(BF16).reshape(nz, count, columns)
    parts = lax.all_to_all(jnp.concatenate([both, fresh], axis=1), "z", 0, 0, tiled=True)

    past = [values[:, :, :group].transpose(1, 2, 0, 3) for values in past]
    return pl.pallas_call(
        functools.partial(finish_kernel, factor),
        in_specs=[VMEM] * 6,
        out_specs=[VMEM] * 2,
        out_shape=[
            jax.ShapeDtypeStruct(weight.shape, BF16),
            jax.ShapeDtypeStruct(queries.shape, BF16),
        ],
        name="finish",
    )(weight, queries, *past, parts)


def solution(mesh):
    names = ("y", "z", "xh", "xl", "c")
    fine = Mesh(np.asarray(mesh.devices).reshape(4, 8, 2, 2, 2), names)
    fsdp, tp = names[:3], names[3:]
    in_specs = (
        P(names, None),
        P(fsdp, tp),
        P(fsdp, tp),
        P(fsdp, None),
        P(fsdp, tp),
        P(fsdp, None, tp),
        P(fsdp),
    )
    out_specs = (P(fsdp, tp), P(fsdp, tp))
    return jax.shard_map(local, mesh=fine, in_specs=in_specs, out_specs=out_specs, check_vma=False)
```

```python
import functools
import math

import jax
import jax.numpy as jnp
import numpy as np
from jax import lax
from jax.experimental import pallas as pl
from jax.experimental.pallas import tpu as pltpu
from jax.sharding import Mesh
from jax.sharding import PartitionSpec as P

KVH = 8
HD = 128
F32 = jnp.float32
BF16 = jnp.bfloat16
X = ("xh", "xl")
VMEM = pl.BlockSpec(memory_space=pltpu.VMEM)


def shift(value, axis, size, by):
    return lax.ppermute(value, axis, [(i, (i + by) % size) for i in range(size)])


def swap(value, axis, size, bits):
    return lax.ppermute(value, axis, [(i, i ^ bits) for i in range(size)])


def pick(array, index, axis=0):
    return lax.dynamic_index_in_dim(array, index, axis, keepdims=False)


def add(a, b):
    return (a.astype(F32) + b.astype(F32)).astype(BF16)


def product_kernel(rows, place, a_ref, b_ref, ca_ref, cb_ref, *outs):
    values = jnp.concatenate([a_ref[...], b_ref[...]], axis=0)
    cots = jnp.concatenate([ca_ref[...], cb_ref[...]], axis=0)
    store(rows, place, tokens_by(values, cots).astype(BF16), outs)


def rest_kernel(rows, place, head_ref, b_ref, cb_ref, *outs):
    total = tokens_by(b_ref[...], cb_ref[...]) + head_ref[...].astype(F32)
    store(rows, place, total.astype(BF16), outs)


def head_kernel(place, a_ref, ca_ref, out_ref):
    out_ref[...] = tokens_by(a_ref[...], ca_ref[...]).astype(BF16)


def tokens_by(values, cots):
    return lax.dot_general(values, cots, (((0,), (0,)), ((), ())), preferred_element_type=F32)


def store(rows, place, total, outs):
    by_y, near, far = outs[:4], outs[4:6], outs[6:]
    turn = pl.program_id(0)
    part = total.shape[1] // 2
    pieces = total.shape[0] // rows
    for k in range(4):

        @pl.when(turn == k)
        def _(k=k):
            for i in range(pieces):
                here = slice(i // 2 * rows, (i // 2 + 1) * rows)
                by_y[k][i % 2, here, :] = total[i * rows : (i + 1) * rows, :part]

    for flip in (0, 1):

        @pl.when(place[1] == flip)
        def _(flip=flip):
            for i in range(pieces):
                half, j = divmod(i // 2, pieces // 4)
                out = (near if i % 2 == flip else far)[half]
                out[0, j * rows : (j + 1) * rows, :] = total[i * rows : (i + 1) * rows, part:]


def product(rows, place, own, other, cots, head=None):
    tokens, width = own.shape
    columns = cots.shape[2]
    part = columns // 2
    tall = width // 4
    token_spec = pl.BlockSpec((tokens, tall), lambda t, place: (0, (place[0] + t) % 4))
    first_cot = pl.BlockSpec((None, tokens, columns), lambda t, place: (place[2], 0, 0))
    second_cot = pl.BlockSpec((None, tokens, columns), lambda t, place: (place[2] ^ 1, 0, 0))
    head_spec = pl.BlockSpec((tall, columns), lambda t, place: ((place[0] + t) % 4, 0))
    y_spec = pl.BlockSpec((2, tall // 2, part), lambda t, place: (0, 0, 0))
    y_shape = jax.ShapeDtypeStruct((2, tall // 2, part), BF16)
    x_spec = pl.BlockSpec((1, tall // 4, part), lambda t, place: ((place[0] + t) % 4, 0, 0))
    x_shape = jax.ShapeDtypeStruct((4, tall // 4, part), BF16)
    out_specs, out_shape = [y_spec] * 4 + [x_spec] * 4, [y_shape] * 4 + [x_shape] * 4
    kernel, name, share = functools.partial(product_kernel, rows), "product", 2
    in_specs, args = [token_spec, token_spec, first_cot, second_cot], (own, other, cots, cots)
    if head is not None:
        kernel, name, share = functools.partial(rest_kernel, rows), "rest", 1
        in_specs, args = [head_spec, token_spec, second_cot], (head, other, cots)
    elif other is None:
        kernel, name, share = head_kernel, "head", 1
        in_specs, args = [token_spec, first_cot], (own, cots)
        out_specs, out_shape = head_spec, jax.ShapeDtypeStruct((width, columns), BF16)
    return pl.pallas_call(
        kernel,
        grid_spec=pltpu.PrefetchScalarGridSpec(
            num_scalar_prefetch=1, grid=(4,), in_specs=in_specs, out_specs=out_specs
        ),
        out_shape=out_shape,
        compiler_params=pltpu.CompilerParams(vmem_limit_bytes=32 << 20),
        cost_estimate=pl.CostEstimate(
            flops=2 * share * tokens * width * columns,
            bytes_accessed=6 * tokens * width,
            transcendentals=0,
        ),
        name=name,
    )(place, *args)


def past_kernel(heads, lengths, query_ref, cache_ref, sum_ref, top_ref, mass_ref):
    span = cache_ref.shape[1]
    live = lax.broadcasted_iota(jnp.int32, (8, span), 1) < lengths[pl.program_id(0)]
    for j in range(heads):
        keys = cache_ref[0, :, 2 * j * HD : (2 * j + 1) * HD]
        values = cache_ref[0, :, (2 * j + 1) * HD : (2 * j + 2) * HD]
        scores = lax.dot_general(
            query_ref[0, j], keys, (((1,), (1,)), ((), ())), preferred_element_type=F32
        ) / math.sqrt(HD)
        scores = jnp.where(live, scores, jnp.float32(-1e30))
        top = jnp.max(scores, axis=1, keepdims=True)
        weights = jnp.exp(scores - top)
        mass = jnp.sum(weights, axis=1, keepdims=True)
        sum_ref[0, j] = jnp.dot(weights.astype(BF16), values, preferred_element_type=F32)
        top_ref[0, j] = jnp.broadcast_to(top, (8, HD))
        mass_ref[0, j] = jnp.broadcast_to(mass, (8, HD))


def attend_past(query, cache, lengths):
    rows, heads = query.shape[:2]
    span, columns = cache.shape[1:]
    small = pl.BlockSpec((1, heads, 8, HD), lambda r, lengths: (r, 0, 0, 0))
    shape = jax.ShapeDtypeStruct((rows, heads, 8, HD), F32)
    return pl.pallas_call(
        functools.partial(past_kernel, heads),
        grid_spec=pltpu.PrefetchScalarGridSpec(
            num_scalar_prefetch=1,
            grid=(rows,),
            in_specs=[small, pl.BlockSpec((1, span, columns), lambda r, lengths: (r, 0, 0))],
            out_specs=[small] * 3,
        ),
        out_shape=[shape] * 3,
        compiler_params=pltpu.CompilerParams(vmem_limit_bytes=24 << 20),
        cost_estimate=pl.CostEstimate(
            flops=32 * rows * span * columns,
            bytes_accessed=2 * rows * span * columns,
            transcendentals=8 * rows * heads * span,
        ),
        name="past",
    )(lengths, query, cache)


def finish_kernel(
    factor, weight_ref, query_ref, sum_ref, top_ref, mass_ref, parts_ref, weight_out, attention_out
):
    rows = weight_ref.shape[0]
    total = parts_ref[0].astype(F32)
    for k in range(1, parts_ref.shape[0]):
        total += parts_ref[k].astype(F32)
    weight_out[...] = (weight_ref[...].astype(F32) - factor * total[:rows]).astype(BF16)
    fresh = total[rows:].astype(BF16).astype(F32)
    heads, group = sum_ref.shape[:2]
    for j in range(heads):
        key = fresh[:, 2 * j * HD : (2 * j + 1) * HD]
        value = fresh[:, (2 * j + 1) * HD : (2 * j + 2) * HD]
        for g in range(group):
            here = slice((j * group + g) * HD, (j * group + g + 1) * HD)
            query = query_ref[:, here].astype(F32)
            newest = jnp.sum(query * key, axis=1, keepdims=True) / math.sqrt(HD)
            old = top_ref[j, g]
            top = jnp.maximum(old, newest)
            past = jnp.exp(old - top)
            new = jnp.exp(newest - top)
            mixed = (sum_ref[j, g] * past + new * value) / (mass_ref[j, g] * past + new)
            attention_out[:, here] = mixed.astype(BF16)


def local(tokens_in, cotangent, weight, hidden_rows, queries, cache, lengths):
    y, z, xh, xl, c = (lax.axis_index(name) for name in ("y", "z", "xh", "xl", "c"))
    ny, nz, nh, nl, nc = (lax.axis_size(name) for name in ("y", "z", "xh", "xl", "c"))
    x = xh * nl + xl
    nx = nh * nl
    tokens, width = tokens_in.shape
    columns = cotangent.shape[1]
    part = columns // 2
    rows = weight.shape[0]
    factor = 0.01 / math.sqrt(tokens * nc * nl * nh * ny * nz)

    heads = KVH // (nl * nc)
    count = queries.shape[0]
    query = queries.reshape(count, heads, -1, HD)
    group = query.shape[2]
    query = jnp.pad(query, ((0, 0), (0, 0), (0, 8 - group), (0, 0)))

    other_tokens = swap(tokens_in, "c", nc, 1)
    blocks = cotangent.reshape(nl, nc, tokens, columns)
    got = swap(pick(blocks, 1 - xl), "xl", nl, 1)

    held = hidden_rows.reshape(count, ny, nz, nh, rows).transpose(3, 1, 0, 2, 4)
    held = held.reshape(nh, ny, count, nz * rows)
    ours, theirs = pick(held, xh), swap(pick(held, 1 - xh), "xh", nh, 1)
    held = jnp.concatenate(
        [jnp.where(xh == 0, ours, theirs), jnp.where(xh == 0, theirs, ours)], axis=1
    )

    place = jnp.stack([y, xh, xl * nc + c]).astype(jnp.int32)
    own_cots = cotangent.reshape(nl * nc, tokens, columns)
    head = product(rows, place, tokens_in, None, own_cots)
    own = product(rows, place, tokens_in, other_tokens, own_cots, head)
    own_y, (own_x0a, own_x0b, own_x2a, own_x2b) = own[:4], own[4:]
    up = shift(own_y[2], "y", ny, 1)
    down = shift(own_y[3], "y", ny, -1)
    up_x = shift(own_x2a, X, nx, 1)
    down_x = shift(own_x2b, X, nx, -1)

    place = jnp.stack([y, jnp.where(xl == 0, xh, 1 - xh), c]).astype(jnp.int32)
    oth = product(rows, place, tokens_in, other_tokens, got)
    oth_y, (oth_x1a, oth_x1b, oth_x3a, oth_x3b) = oth[:4], oth[4:]
    oth_y2, up, down, query = lax.optimization_barrier((oth_y[2], up, down, query))
    oth_x1b, up_x, down_x = lax.optimization_barrier((oth_x1b, up_x, down_x))
    far = shift(oth_y2, "y", ny, -1)
    past = attend_past(query, cache, lengths)

    far, held = lax.optimization_barrier((far, held))
    held = jnp.broadcast_to(held[:, None], (ny, nz, *held.shape[1:]))
    held = lax.all_to_all(
        held.reshape(ny * nz, nh * count, nz * rows), ("y", "z"), 0, 0, tiled=True
    ).reshape(-1, nz * rows)

    oth_up = shift(oth_y[1], "y", ny, 1)
    own_up = shift(add(own_y[1], up), "y", ny, 1)
    up_b = shift(oth_x1b, X, nx, 1)
    down_a = shift(oth_x3a, X, nx, -1)
    far, oth_up, up_b, down_a = lax.optimization_barrier((far, oth_up, up_b, down_a))
    oth_down = shift(add(oth_y[3], far), "y", ny, -1)
    up_a = shift(add(oth_x1a, up_x), X, nx, 1)
    down_b = shift(add(oth_x3b, down_x), X, nx, -1)

    up_a, up_b, down_a, down_b, own_up = lax.optimization_barrier(
        (up_a, up_b, down_a, down_b, own_up)
    )

    def after_y(k):
        index = ((x + k) % nx) // nl
        terms = (oth_y[0], oth_up, oth_down) if k % 2 else (own_y[0], own_up, down)
        return sum(pick(term, index).astype(F32) for term in terms)

    by_y = (
        jnp.stack([own_x0a, own_x0b], axis=1).astype(F32)
        + jnp.stack([up_a, up_b], axis=1).astype(F32)
        + jnp.stack([down_a, down_b], axis=1).astype(F32)
    ).astype(BF16)
    by_y = by_y.reshape(ny, nz * rows, part)
    first, second = after_y(0), pick(by_y, y).astype(F32)
    for k in (2, 1, 3):
        first += shift(after_y(k).astype(BF16), X, nx, k).astype(F32)
        second += shift(pick(by_y, (y + k) % ny), "y", ny, k).astype(F32)
    both = jnp.concatenate([first.astype(BF16), second.astype(BF16)], axis=1)
    both = both.reshape(nz, rows, columns)

    here = (lax.broadcasted_iota(jnp.int32, (nz, 1, 1), 0) == z).astype(F32)
    update = here * weight.astype(F32) - factor * both.astype(F32)
    update = update.astype(BF16).reshape(nz * rows, columns)
    fresh = jnp.dot(held, update, preferred_element_type=F32).astype(BF16)
    fresh = fresh.reshape(ny, nz, nh, count, columns).transpose(0, 2, 1, 3, 4)
    fresh = lax.all_to_all(
        fresh.reshape(ny * nh, nz * count, columns), ("y", "xh"), 0, 0, tiled=True
    )
    fresh = jnp.sum(fresh.astype(F32), axis=0).astype(BF16).reshape(nz, count, columns)
    parts = lax.all_to_all(jnp.concatenate([both, fresh], axis=1), "z", 0, 0, tiled=True)

    past = [values[:, :, :group].transpose(1, 2, 0, 3) for values in past]
    return pl.pallas_call(
        functools.partial(finish_kernel, factor),
        in_specs=[VMEM] * 6,
        out_specs=[VMEM] * 2,
        out_shape=[
            jax.ShapeDtypeStruct(weight.shape, BF16),
            jax.ShapeDtypeStruct(queries.shape, BF16),
        ],
        name="finish",
    )(weight, queries, *past, parts)


def solution(mesh):
    names = ("y", "z", "xh", "xl", "c")
    fine = Mesh(np.asarray(mesh.devices).reshape(4, 8, 2, 2, 2), names)
    fsdp, tp = names[:3], names[3:]
    in_specs = (
        P(names, None),
        P(fsdp, tp),
        P(fsdp, tp),
        P(fsdp, None),
        P(fsdp, tp),
        P(fsdp, None, tp),
        P(fsdp),
    )
    out_specs = (P(fsdp, tp), P(fsdp, tp))
    return jax.shard_map(local, mesh=fine, in_specs=in_specs, out_specs=out_specs, check_vma=False)
```
